128 devices in a mesh: seq: 16 (over z, x), mp: 8 (over y, core).
Axes of the slice: x: 4, y: 4, z: 4, core: 2. Of those that a mesh axis runs over, the one named last changes fastest.
Arguments:
- query_raw: bfloat16 [8, 2048, 6144], P('mp', 'seq'), may hold values from -480 to 480
- key_raw: bfloat16 [8, 2048, 6144], P('mp', 'seq'), may hold values from -480 to 480
- value_rows: bfloat16 [8, 2048, 6144], P('mp', 'seq'), may hold values from -12 to 12
- out_grads: bfloat16 [8, 2048, 6144], P('mp', 'seq'), may hold values from -16 to 16
- image_ids: int32 [8, 2048], P('mp', 'seq'), may hold values from 0 to 7, never falling along the last dimension, each value on 1 to 1024 neighbouring positions
- qk_gains: float32 [2, 128], replicated, may hold values from 0.5 to 6
Outputs:
- query_grads: bfloat16 [8, 2048, 6144], P('mp', 'seq')
- key_grads: bfloat16 [8, 2048, 6144], P('mp', 'seq')
- value_grads: bfloat16 [8, 2048, 6144], P('mp', 'seq')
- gain_grads: float32 [2, 128], replicated
The draws below stay inside these ranges and needn't reach their ends.
Inputs may be any that keep to these rules, and one draw needn't show every extreme that they name: `image_ids`: ids never fall along a row, every id below 8 occurs in every row, and in every row one image spans exactly 1024 patches.
All inputs are finite; a program needn't handle non-finite values.
Results may differ from the reference program's by a relative error of at most 0.004.
The reference program's roundings to bfloat16 on the way (of `rounded_weights` and `score_grads`) count: a program that leaves them out, or rounds other values in their place, can miss the bound.
Values may be sent and summed in bfloat16 or wider, within the bound.
A program may use at most 192 MiB of HBM per device.

```python
import math
import jax
import jax.numpy as jnp
import numpy as np
from jax import lax

HEADS = 48
HD = 128
IMGS = 8
L = 2048
ROWS = 8
MOST = 1024


def draw_query_raw(key, part):
    own_key = jax.random.fold_in(key, 1)
    own_draw = jnp.clip(jax.random.normal(own_key, (ROWS, L, HEADS, HD), jnp.float32), -4.5, 4.5)
    return own_draw.reshape(ROWS, L, HEADS * HD).astype(jnp.bfloat16)


def draw_key_raw(key, part):
    own_key = jax.random.fold_in(key, 2)
    own_draw = jnp.clip(jax.random.normal(own_key, (ROWS, L, HEADS, HD), jnp.float32), -4.5, 4.5)
    return own_draw.reshape(ROWS, L, HEADS * HD).astype(jnp.bfloat16)


def draw_out_grads(key, part):
    own_key = jax.random.fold_in(key, 3)
    place_frac = (jnp.arange(ROWS)[:, None] * L + jnp.arange(L)[None, :]).astype(jnp.float32) / (ROWS * L - 1)
    normal_draw = jnp.clip(jax.random.normal(own_key, (ROWS, L, HEADS * HD), jnp.float32), -4.5, 4.5)
    return (normal_draw * (1.0 + 2.0 * place_frac)[:, :, None]).astype(jnp.bfloat16)


def draw_qk_gains(key, part):
    own_key = jax.random.fold_in(key, 4)
    return jax.random.uniform(own_key, (2, HD), jnp.float32, 0.5, 1.5)


def levels(stream_key, shape, split, low, largest):
    factor_of = 1.0
    for position, blocks in split:
        draws = jax.random.uniform(jax.random.fold_in(jax.random.fold_in(stream_key, 6), position), (blocks,), jnp.float32, low / len(split), largest / len(split))
        factor_of = factor_of * jnp.repeat(jnp.exp(draws), shape[position] // blocks).reshape((-1,) + (1,) * (len(shape) - 1 - position))
    return factor_of


def profile(amount, total, bound, skew):
    loads = [(1 << 20) // math.isqrt(grade ** skew) + 1 for grade in range(2, amount + 1)]
    rest, counts = total - bound - (amount - 1), [1] * (amount - 1)
    while rest > 0:
        candidates = [i for i in range(amount - 1) if counts[i] < bound]
        whole, budget = sum([loads[i] for i in candidates]), rest
        for i in candidates:
            addition = min(bound - counts[i], max(1, budget * loads[i] // whole), rest)
            counts[i] = counts[i] + addition
            rest = rest - addition
    return np.array([bound] + counts)


def uneven_parts(stream_key, amount, total, most, skew):
    if amount == 2:
        one = jax.random.randint(stream_key, (), max(1, total - most), min(most, total - 1) + 1)
        return jnp.stack([one, total - one])
    sizes = jnp.asarray(profile(amount, total, most, skew), jnp.int32)
    couples = (amount - 1) // 2
    source_of, receiver = sizes[1:1 + 2 * couples:2], sizes[2:2 + 2 * couples:2]
    room = jnp.minimum(source_of - 1, most - receiver)
    moved = jax.random.randint(jax.random.fold_in(stream_key, 1), (couples,), 0, 1 << 20) % (room + 1)
    sizes = sizes.at[1:1 + 2 * couples:2].set(source_of - moved).at[2:2 + 2 * couples:2].set(receiver + moved)
    return sizes[jax.random.permutation(jax.random.fold_in(stream_key, 2), amount)]


def noise(stream_key, extent, spread, limit, split=(), held_as=jnp.bfloat16):
    values = spread * jax.random.normal(stream_key, extent, jnp.float32)
    if split:
        values = values * levels(stream_key, extent, split, -0.22, 0.18)
    return jnp.clip(values, -limit, limit).astype(held_as)


def setup_inputs(seed: int = 0) -> dict:
    arg_keys = jax.random.split(jax.random.key(seed), 7)
    query_raw = draw_query_raw(jax.random.fold_in(arg_keys[6], 71), 0)
    key_raw = draw_key_raw(jax.random.fold_in(arg_keys[6], 71), 0)
    value_rows = noise(arg_keys[2], (ROWS, L, HEADS * HD), 2.0, 12.0, ((0, 8), (1, 16)))
    out_grads = draw_out_grads(jax.random.fold_in(arg_keys[6], 71), 0)
    image_ids = jax.vmap(lambda own: jnp.searchsorted(jnp.cumsum(uneven_parts(own, IMGS, L, MOST, 2)), jnp.arange(L), side="right"))(jax.random.split(arg_keys[4], ROWS)).reshape((ROWS, L)).astype(jnp.int32)
    qk_gains = draw_qk_gains(jax.random.fold_in(arg_keys[6], 71), 0)
    return dict(query_raw=query_raw, key_raw=key_raw, value_rows=value_rows, out_grads=out_grads, image_ids=image_ids, qk_gains=qk_gains)


EPSILON = 1e-06

def norm_forward(source, gain_row):
    as_float = source.astype(jnp.float32)
    centered = as_float - lax.optimization_barrier(jnp.mean(as_float, axis=-1, keepdims=True))
    inv_std = lax.rsqrt(lax.optimization_barrier(jnp.mean(centered * centered, axis=-1, keepdims=True)) + EPSILON)
    unit_vals = centered * inv_std
    return ((unit_vals * gain_row).astype(jnp.bfloat16), unit_vals, inv_std)

def norm_backward(tangent, unit_vals, inv_std, gain_row):
    scaled_up = tangent * gain_row
    adjusted = scaled_up - lax.optimization_barrier(jnp.mean(scaled_up, axis=-1, keepdims=True)) - unit_vals * lax.optimization_barrier(jnp.mean(scaled_up * unit_vals, axis=-1, keepdims=True))
    return (inv_std * adjusted).astype(jnp.bfloat16)

def head_backward(head_query, head_key, head_value, head_grad, same_image, gains_pair):
    scaling = HD ** (-0.5)
    query_norm, query_unit, query_inv = norm_forward(head_query, gains_pair[0])
    key_norm, key_unit, key_inv = norm_forward(head_key, gains_pair[1])
    scores = jnp.dot(query_norm, key_norm.T, preferred_element_type=jnp.float32) * scaling
    scores = jnp.where(same_image, scores, -jnp.inf)
    row_max = lax.optimization_barrier(jnp.max(scores, axis=-1, keepdims=True))
    exp_scores = jnp.exp(scores - row_max)
    attn_weights = exp_scores / lax.optimization_barrier(jnp.sum(exp_scores, axis=-1, keepdims=True))
    rounded_weights = attn_weights.astype(jnp.bfloat16)
    attn_output = jnp.dot(rounded_weights, head_value, preferred_element_type=jnp.float32)
    row_delta = lax.optimization_barrier(jnp.sum(head_grad.astype(jnp.float32) * attn_output, axis=-1, keepdims=True))
    weight_grads = jnp.dot(head_grad, head_value.T, preferred_element_type=jnp.float32)
    score_grads = (attn_weights * (weight_grads - row_delta)).astype(jnp.bfloat16)
    query_tangent = scaling * jnp.dot(score_grads, key_norm, preferred_element_type=jnp.float32)
    key_tangent = scaling * jnp.dot(score_grads.T, query_norm, preferred_element_type=jnp.float32)
    value_grads = jnp.dot(rounded_weights.T, head_grad, preferred_element_type=jnp.float32).astype(jnp.bfloat16)
    query_grads = norm_backward(query_tangent, query_unit, query_inv, gains_pair[0])
    key_grads = norm_backward(key_tangent, key_unit, key_inv, gains_pair[1])
    gain_terms = jnp.stack([lax.optimization_barrier(jnp.sum(query_tangent * query_unit, axis=0)), lax.optimization_barrier(jnp.sum(key_tangent * key_unit, axis=0))])
    return (query_grads, key_grads, value_grads, gain_terms)

def reference(query_raw, key_raw, value_rows, out_grads, image_ids, qk_gains):

    def split_heads(source):
        return jnp.moveaxis(source.reshape(L, HEADS, HD), 1, 0)

    def join_heads(source):
        return jnp.moveaxis(source, 0, 1).reshape(L, HEADS * HD)

    def one_row(row_items):
        row_query, row_key, row_value, row_grad, row_images = row_items
        same_image = row_images[:, None] == row_images[None, :]

        def one_head(head_parts):
            return head_backward(head_parts[0], head_parts[1], head_parts[2], head_parts[3], same_image, qk_gains)
        query_part, key_part, value_part, term_part = lax.map(one_head, (split_heads(row_query), split_heads(row_key), split_heads(row_value), split_heads(row_grad)))
        return (join_heads(query_part), join_heads(key_part), join_heads(value_part), lax.optimization_barrier(jnp.sum(term_part, axis=0)))
    query_grads, key_grads, value_grads, row_terms = lax.map(one_row, (query_raw, key_raw, value_rows, out_grads, image_ids))
    gain_grads = lax.optimization_barrier(jnp.sum(row_terms, axis=0)) * (L * HEADS) ** (-0.5)
    return (query_grads, key_grads, value_grads, gain_grads)
```

```python
import functools
import math

import jax
import jax.numpy as jnp
from jax import lax
from jax.experimental import pallas as pl
from jax.experimental.pallas import tpu as pltpu
from jax.sharding import PartitionSpec as P

MESH = pl.DeviceIdType.MESH
EPSILON = 1e-06
BAN = -32768.0
CLASSES = 8
QT = 256
KT = 512
RT = 256
MOST = 1024
F32 = jnp.float32
BF16 = jnp.bfloat16


def contract_last(a, b):
    return lax.dot_general(a, b, (((1,), (1,)), ((), ())), preferred_element_type=F32)


def matmul(a, b):
    return lax.dot_general(a, b, (((1,), (0,)), ((), ())), preferred_element_type=F32)


def fold(x):
    return x.reshape(x.shape[0] // 8, 8, x.shape[1])


def kernel(
    n, m, heads, tok, hd,
    q_hbm, k_hbm, v_hbm, g_hbm, ids_ref, gains_ref,
    oq_hbm, ok_hbm, ov_hbm, gain_ref,
    in_buf, out_buf, id_src, id_buf, q_aug, k_aug, k_turned, unit_buf, inv_buf,
    s_buf, w_buf, p_buf, dk_acc, dv_acc, gain_acc, gain_seq, gain_mp,
    in_send, in_recv, id_send, id_recv, out_send, out_recv, gain_send, gain_recv,
):
    seq, mp = lax.axis_index("seq"), lax.axis_index("mp")
    length = n * tok
    side = math.isqrt(n)
    scaling = hd ** (-0.5)
    exponent = scaling * math.log2(math.e)

    def partner(i):
        z = lax.rem(seq // side + i // side, side)
        x = lax.rem(lax.rem(seq, side) + lax.rem(i, side), side)
        return z * side + x

    def mp_partner(i):
        return lax.rem(mp + i, m)

    def remote(src, dst, send, recv, to_seq, to_mp):
        return pltpu.make_async_remote_copy(
            src_ref=src, dst_ref=dst, send_sem=send, recv_sem=recv,
            device_id=(to_seq, to_mp), device_id_type=MESH,
        )

    barrier = pltpu.get_barrier_semaphore()

    def greet_seq(i, c):
        pl.semaphore_signal(barrier, inc=1, device_id=(partner(i), mp), device_id_type=MESH)
        return c

    def greet_mp(i, c):
        pl.semaphore_signal(barrier, inc=1, device_id=(seq, mp_partner(i)), device_id_type=MESH)
        return c

    lax.fori_loop(1, n, greet_seq, 0)
    lax.fori_loop(1, m, greet_mp, 0)
    id_src[...] = jnp.broadcast_to(ids_ref[...], (8, tok))
    id_buf[pl.ds(pl.multiple_of(seq * 8, 8), 8), :] = jnp.broadcast_to(ids_ref[...], (8, tok))
    pl.semaphore_wait(barrier, n - 1 + m - 1)

    def send_ids(i, c):
        remote(
            id_src, id_buf.at[pl.ds(pl.multiple_of(seq * 8, 8), 8)],
            id_send.at[0], id_recv.at[0], partner(i), mp,
        ).start()
        return c

    lax.fori_loop(1, n, send_ids, 0)
    sources = (q_hbm, k_hbm, v_hbm, g_hbm)

    def in_rows(h, a, s):
        return pl.ds(pl.multiple_of(((h * 4 + a) * n + s) * tok, tok), tok)

    def lanes(owner, h):
        return pl.ds(pl.multiple_of((owner * heads + h) * hd, hd), hd)

    def send_head(h, c):
        for a in range(4):
            pltpu.make_async_copy(
                sources[a].at[0, :, lanes(seq, h)], in_buf.at[in_rows(h, a, seq)], in_recv.at[h]
            ).start()

            def send_one(i, c, a=a):
                to = partner(i)
                remote(
                    sources[a].at[0, :, lanes(to, h)], in_buf.at[in_rows(h, a, seq)],
                    in_send.at[0], in_recv.at[h], to, mp,
                ).start()
                return c

            lax.fori_loop(1, n, send_one, 0)
        return c

    lax.fori_loop(0, heads, send_head, 0)

    ids_got = id_buf.at[pl.ds(0, (n - 1) * 8)]
    pltpu.make_async_copy(ids_got, ids_got, id_recv.at[0]).wait()
    lane = lax.broadcasted_iota(jnp.int32, (tok, hd), 1)

    def features(s, c):
        row = id_buf[pl.ds(pl.multiple_of(s * 8, 8), 8), :].astype(F32)[:1]
        image = jnp.transpose(jnp.broadcast_to(row, (hd, tok))).astype(jnp.int32)
        same = image == lane
        rows = pl.ds(pl.multiple_of(s * tok, tok), tok)
        q_aug[rows, hd:] = jnp.where(same, 1.0, 0.0).astype(BF16)
        k_aug[rows, hd:] = jnp.where(jnp.logical_and(lane < CLASSES, ~same), BAN, 0.0).astype(BF16)
        return c

    lax.fori_loop(0, n, features, 0)
    gain_acc[...] = jnp.zeros_like(gain_acc)

    def mean(x):
        return jnp.sum(x, axis=-1, keepdims=True) * (1.0 / hd)

    def norm_backward(tangent, unit, inv, gain_row):
        u = tangent * gain_row
        return (inv * (u - mean(u) - unit * mean(u * unit))).astype(BF16)

    def one_head(h, c):
        base = pl.multiple_of(h * 4 * length, tok)
        out_base = pl.multiple_of(h * 3 * length, tok)
        whole = in_buf.at[pl.ds(base, 4 * length)]
        pltpu.make_async_copy(whole, whole, in_recv.at[h]).wait()

        def norm(t, c):
            for a, held in ((0, q_aug), (1, k_aug)):
                rows = pl.ds(pl.multiple_of(t * RT, RT), RT)
                side_rows = pl.ds(pl.multiple_of(a * length + t * RT, RT), RT)
                x = in_buf[pl.ds(pl.multiple_of(base + a * length + t * RT, RT), RT), :].astype(F32)
                centered = x - mean(x)
                inv = lax.rsqrt(mean(centered * centered) + EPSILON)
                unit = centered * inv
                normed = unit * gains_ref[a : a + 1, :]
                held[rows, :hd] = normed.astype(BF16)
                unit_buf[side_rows, :] = unit
                inv_buf[side_rows, :] = jnp.broadcast_to(inv, (RT, hd))
                if a == 1:
                    k_turned[:, rows] = jnp.transpose(normed).astype(BF16)
                    dk_acc[rows, :] = jnp.zeros((RT, hd), F32)
                    dv_acc[rows, :] = jnp.zeros((RT, hd), F32)
            return c

        lax.fori_loop(0, length // RT, norm, 0)

        def panel(i, c):
            q_rows = pl.ds(pl.multiple_of(i * QT, QT), QT)
            q_tile = q_aug[q_rows, :]
            q_plain = q_aug[q_rows, :hd]
            g_tile = in_buf[pl.ds(pl.multiple_of(base + 3 * length + i * QT, QT), QT), :]
            first = jnp.maximum(i * QT - (MOST - 1), 0) // KT
            last = jnp.minimum(i * QT + QT - 1 + MOST - 1, length - 1) // KT + 1

            def chunk(j):
                return pl.ds(pl.multiple_of(j * KT, KT), KT)

            def scores(j, top):
                rows = chunk(j)
                s = contract_last(k_aug[rows, :], q_tile)
                s_buf[rows, :] = s
                v = in_buf[pl.ds(pl.multiple_of(base + 2 * length + j * KT, KT), KT), :]
                w_buf[rows, :] = contract_last(v, g_tile)
                return jnp.maximum(top, jnp.max(fold(s), axis=0))

            top = lax.fori_loop(first, last, scores, jnp.full((8, QT), -jnp.inf, F32))
            top = jnp.max(top, axis=0, keepdims=True)

            def exps(j, total):
                rows = chunk(j)
                e = jnp.exp2((s_buf[rows, :] - top) * exponent)
                s_buf[rows, :] = e
                return total + jnp.sum(fold(e), axis=0)

            total = lax.fori_loop(first, last, exps, jnp.zeros((8, QT), F32))
            over = 1.0 / jnp.sum(total, axis=0, keepdims=True)

            def weights(j, delta):
                rows = chunk(j)
                w = s_buf[rows, :] * over
                s_buf[rows, :] = w
                p = w.astype(BF16)
                p_buf[rows, :] = p
                return delta + jnp.sum(fold(p.astype(F32) * w_buf[rows, :]), axis=0)

            delta = lax.fori_loop(first, last, weights, jnp.zeros((8, QT), F32))
            delta = jnp.sum(delta, axis=0, keepdims=True)

            def grads(j, dq):
                rows = chunk(j)
                ds = (s_buf[rows, :] * (w_buf[rows, :] - delta)).astype(BF16)
                dv_acc[rows, :] += matmul(p_buf[rows, :], g_tile)
                dk_acc[rows, :] += matmul(ds, q_plain)
                return dq + matmul(k_turned[:, rows], ds)

            dq = lax.fori_loop(first, last, grads, jnp.zeros((hd, QT), F32))
            tangent = jnp.transpose(dq) * scaling
            unit = unit_buf[q_rows, :]
            out_rows = pl.ds(pl.multiple_of(out_base + i * QT, QT), QT)
            out_buf[out_rows, :] = norm_backward(
                tangent, unit, inv_buf[q_rows, :], gains_ref[0:1, :]
            )
            gain_acc[0:8, :] += jnp.sum(fold(tangent * unit), axis=0)
            return c

        lax.fori_loop(0, length // QT, panel, 0)

        def finish(t, c):
            rows = pl.ds(pl.multiple_of(t * RT, RT), RT)
            side_rows = pl.ds(pl.multiple_of(length + t * RT, RT), RT)
            tangent = dk_acc[rows, :] * scaling
            unit = unit_buf[side_rows, :]
            out_buf[pl.ds(pl.multiple_of(out_base + length + t * RT, RT), RT), :] = norm_backward(
                tangent, unit, inv_buf[side_rows, :], gains_ref[1:2, :]
            )
            gain_acc[8:16, :] += jnp.sum(fold(tangent * unit), axis=0)
            out_buf[pl.ds(pl.multiple_of(out_base + 2 * length + t * RT, RT), RT), :] = dv_acc[
                rows, :
            ].astype(BF16)
            return c

        lax.fori_loop(0, length // RT, finish, 0)

        @pl.when(h == heads - 1)
        def _():
            terms = [jnp.sum(gain_acc[8 * a : 8 * a + 8, :], axis=0, keepdims=True) for a in (0, 1)]
            own = jnp.concatenate(terms + [jnp.zeros((6, hd), F32)], axis=0)
            gain_acc[16:24, :] = own
            slot = pl.ds(pl.multiple_of(seq * 8, 8), 8)
            gain_seq[slot, :] = own

            def send_terms(i, c):
                remote(
                    gain_acc.at[pl.ds(16, 8)], gain_seq.at[slot],
                    gain_send.at[0], gain_recv.at[0], partner(i), mp,
                ).start()
                return c

            lax.fori_loop(1, n, send_terms, 0)

        targets = (oq_hbm, ok_hbm, ov_hbm)

        def out_rows(a, s):
            return pl.ds(pl.multiple_of(((h * 3 + a) * n + s) * tok, tok), tok)

        for a in range(3):
            pltpu.make_async_copy(
                out_buf.at[out_rows(a, seq)], targets[a].at[0, :, lanes(seq, h)], out_recv.at[0]
            ).start()

            def send_one(i, c, a=a):
                to = partner(i)
                remote(
                    out_buf.at[out_rows(a, to)], targets[a].at[0, :, lanes(seq, h)],
                    out_send.at[0], out_recv.at[0], to, mp,
                ).start()
                return c

            lax.fori_loop(1, n, send_one, 0)
        return c

    lax.fori_loop(0, heads, one_head, 0)

    got = gain_seq.at[pl.ds(0, (n - 1) * 8)]
    pltpu.make_async_copy(got, got, gain_recv.at[0]).wait()
    row_sum = jnp.sum(gain_seq[...].reshape(n, 8, hd), axis=0)
    gain_acc[24:32, :] = row_sum
    mp_slot = pl.ds(pl.multiple_of(mp * 8, 8), 8)
    gain_mp[mp_slot, :] = row_sum

    def send_sums(i, c):
        remote(
            gain_acc.at[pl.ds(24, 8)], gain_mp.at[mp_slot],
            gain_send.at[1], gain_recv.at[1], seq, mp_partner(i),
        ).start()
        return c

    lax.fori_loop(1, m, send_sums, 0)
    got = gain_mp.at[pl.ds(0, (m - 1) * 8)]
    pltpu.make_async_copy(got, got, gain_recv.at[1]).wait()
    total = jnp.sum(gain_mp[...].reshape(m, 8, hd), axis=0)
    gain_ref[...] = total[:2] * (length * n * heads) ** (-0.5)

    def drain(ref, sem):
        pltpu.make_async_copy(ref, ref, sem).wait()

    drain(id_buf.at[pl.ds(0, (n - 1) * 8)], id_send.at[0])
    drain(gain_seq.at[pl.ds(0, (n - 1) * 8)], gain_send.at[0])
    drain(gain_mp.at[pl.ds(0, (m - 1) * 8)], gain_send.at[1])
    drain(in_buf.at[pl.ds(0, heads * 4 * (n - 1) * tok)], in_send.at[0])
    drain(out_buf.at[pl.ds(0, heads * 3 * (n - 1) * tok)], out_send.at[0])
    drain(out_buf, out_recv.at[0])


def shards(n, m, query_raw, key_raw, value_rows, out_grads, image_ids, qk_gains):
    tok, width = query_raw.shape[1:]
    hd = qk_gains.shape[1]
    heads = width // hd // n
    length = n * tok
    grad = jax.ShapeDtypeStruct(query_raw.shape, BF16)
    hbm = pl.BlockSpec(memory_space=pl.ANY)
    vmem = pl.BlockSpec(memory_space=pltpu.VMEM)
    dma = pltpu.SemaphoreType.DMA
    return pl.pallas_call(
        functools.partial(kernel, n, m, heads, tok, hd),
        out_shape=(grad, grad, grad, jax.ShapeDtypeStruct((2, hd), F32)),
        in_specs=[hbm, hbm, hbm, hbm, vmem, vmem],
        out_specs=(hbm, hbm, hbm, vmem),
        scratch_shapes=[
            pltpu.VMEM((heads * 4 * length, hd), BF16),
            pltpu.VMEM((heads * 3 * length, hd), BF16),
            pltpu.VMEM((8, tok), jnp.int32),
            pltpu.VMEM((n * 8, tok), jnp.int32),
            pltpu.VMEM((length, 2 * hd), BF16),
            pltpu.VMEM((length, 2 * hd), BF16),
            pltpu.VMEM((hd, length), BF16),
            pltpu.VMEM((2 * length, hd), F32),
            pltpu.VMEM((2 * length, hd), F32),
            pltpu.VMEM((length, QT), F32),
            pltpu.VMEM((length, QT), F32),
            pltpu.VMEM((length, QT), BF16),
            pltpu.VMEM((length, hd), F32),
            pltpu.VMEM((length, hd), F32),
            pltpu.VMEM((32, hd), F32),
            pltpu.VMEM((n * 8, hd), F32),
            pltpu.VMEM((m * 8, hd), F32),
            dma((1,)), dma((heads,)), dma((1,)), dma((1,)), dma((1,)), dma((1,)), dma((2,)), dma((2,)),
        ],
        compiler_params=pltpu.CompilerParams(
            collective_id=0, has_side_effects=True, vmem_limit_bytes=56 * 2**20
        ),
    )(query_raw, key_raw, value_rows, out_grads, image_ids, qk_gains)


def solution(mesh):
    rows = P("mp", "seq", None)
    return jax.shard_map(
        functools.partial(shards, mesh.shape["seq"], mesh.shape["mp"]),
        mesh=mesh,
        in_specs=(rows, rows, rows, rows, P("mp", "seq"), P()),
        out_specs=(rows, rows, rows, P()),
        check_vma=False,
    )
```

```python
import functools
import math

import jax
import jax.numpy as jnp
from jax import lax
from jax.experimental import pallas as pl
from jax.experimental.pallas import tpu as pltpu
from jax.sharding import PartitionSpec as P

MESH = pl.DeviceIdType.MESH
EPSILON = 1e-06
BAN = -32768.0
CLASSES = 8
QT = 512
KT = 512
RT = 1024
MOST = 1024
F32 = jnp.float32
BF16 = jnp.bfloat16


def matmul(a, b):
    return lax.dot_general(a, b, (((1,), (0,)), ((), ())), preferred_element_type=F32)


def fold(x):
    return x.reshape(x.shape[0] // 8, 8, x.shape[1])


def kernel(
    n, m, heads, tok, hd,
    q_hbm, k_hbm, v_hbm, g_hbm, ids_hbm, gains_hbm,
    oq_ref, ok_ref, ov_ref, gain_ref,
    in_buf, out_buf, ids_ref, gains_ref, id_src, id_buf, q_plain, q_turned, g_turned, k_aug, k_turned, unit_buf, inv_buf,
    s_buf, w_buf, p_buf, dk_acc, dv_acc, gain_acc, gain_seq, gain_mp,
    own_sems, in_send, in_recv, id_send, id_recv, out_send, out_recv, gain_send, gain_recv,
):
    seq, mp = lax.axis_index("seq"), lax.axis_index("mp")
    length = n * tok
    side = math.isqrt(n)
    scaling = hd ** (-0.5)
    exponent = scaling * math.log2(math.e)

    def partner(i):
        i = lax.rem(i * 7, n)
        z = lax.rem(seq // side + i // side, side)
        x = lax.rem(lax.rem(seq, side) + lax.rem(i, side), side)
        return z * side + x

    def mp_partner(i):
        return lax.rem(mp + i, m)

    def remote(src, dst, send, recv, to_seq, to_mp):
        return pltpu.make_async_remote_copy(
            src_ref=src, dst_ref=dst, send_sem=send, recv_sem=recv,
            device_id=(to_seq, to_mp), device_id_type=MESH,
        )

    own_ids = pltpu.make_async_copy(ids_hbm, ids_ref, own_sems.at[0])
    own_gains = pltpu.make_async_copy(gains_hbm, gains_ref, own_sems.at[1])
    own_ids.start()
    own_gains.start()
    barrier = pltpu.get_barrier_semaphore()

    def greet_seq(i, c):
        pl.semaphore_signal(barrier, inc=1, device_id=(partner(i), mp), device_id_type=MESH)
        return c

    def greet_mp(i, c):
        pl.semaphore_signal(barrier, inc=1, device_id=(seq, mp_partner(i)), device_id_type=MESH)
        return c

    lax.fori_loop(1, n, greet_seq, 0)
    lax.fori_loop(1, m, greet_mp, 0)
    own_ids.wait()
    own_gains.wait()
    id_src[...] = jnp.broadcast_to(ids_ref[...], (8, tok))
    id_buf[pl.ds(pl.multiple_of(seq * 8, 8), 8), :] = jnp.broadcast_to(ids_ref[...], (8, tok))
    pl.semaphore_wait(barrier, n - 1 + m - 1)

    def send_ids(i, c):
        remote(
            id_src, id_buf.at[pl.ds(pl.multiple_of(seq * 8, 8), 8)],
            id_send.at[0], id_recv.at[0], partner(i), mp,
        ).start()
        return c

    lax.fori_loop(1, n, send_ids, 0)
    sources = (q_hbm, k_hbm, v_hbm, g_hbm)

    def in_rows(h, a, s):
        return pl.ds(pl.multiple_of(((h * 4 + a) * n + s) * tok, tok), tok)

    def lanes(owner, h):
        return pl.ds(pl.multiple_of((owner * heads + h) * hd, hd), hd)

    def send_head(h, c):
        for a in range(4):
            pltpu.make_async_copy(
                sources[a].at[0, :, lanes(seq, h)], in_buf.at[in_rows(h, a, seq)], in_recv.at[h]
            ).start()

            def send_one(i, c, a=a):
                to = partner(i)
                remote(
                    sources[a].at[0, :, lanes(to, h)], in_buf.at[in_rows(h, a, seq)],
                    in_send.at[0], in_recv.at[h], to, mp,
                ).start()
                return c

            lax.fori_loop(1, n, send_one, 0)
        return c

    lax.fori_loop(0, heads, send_head, 0)

    ids_got = id_buf.at[pl.ds(0, (n - 1) * 8)]
    pltpu.make_async_copy(ids_got, ids_got, id_recv.at[0]).wait()
    lane = lax.broadcasted_iota(jnp.int32, (tok, hd), 1)
    level = lax.broadcasted_iota(jnp.int32, (hd, tok), 0)

    def features(s, c):
        row = id_buf[pl.ds(pl.multiple_of(s * 8, 8), 8), :].astype(F32)[:1]
        image = jnp.transpose(jnp.broadcast_to(row, (hd, tok))).astype(jnp.int32)
        rows = pl.ds(pl.multiple_of(s * tok, tok), tok)
        q_turned[hd:, rows] = jnp.where(row.astype(jnp.int32) == level, 1.0, 0.0).astype(BF16)
        k_aug[rows, hd:] = jnp.where(
            jnp.logical_and(lane < CLASSES, image != lane), BAN, 0.0
        ).astype(BF16)
        return c

    lax.fori_loop(0, n, features, 0)
    gain_acc[...] = jnp.zeros_like(gain_acc)

    def mean(x):
        return jnp.sum(x.astype(F32), axis=-1, keepdims=True) * (1.0 / hd)

    def norm_backward(tangent, unit, inv, gain_row):
        u = tangent * gain_row
        return (inv * (u - mean(u) - unit * mean(u * unit))).astype(BF16)

    def one_head(h, c):
        base = pl.multiple_of(h * 4 * length, tok)
        out_base = pl.multiple_of(h * 3 * length, tok)
        whole = in_buf.at[pl.ds(base, 4 * length)]
        pltpu.make_async_copy(whole, whole, in_recv.at[h]).wait()

        def norm(t, c):
            rows = pl.ds(pl.multiple_of(t * RT, RT), RT)

            def arrived(a):
                return in_buf[pl.ds(pl.multiple_of(base + a * length + t * RT, RT), RT), :]

            for a in (0, 1):
                side_rows = pl.ds(pl.multiple_of(a * length + t * RT, RT), RT)
                raw = arrived(a)
                centered = raw.astype(F32) - mean(raw)
                inv = lax.rsqrt(mean(centered * centered) + EPSILON)
                unit = centered * inv
                normed = unit * gains_ref[a : a + 1, :]
                unit_buf[side_rows, :] = unit
                inv_buf[side_rows, :] = jnp.broadcast_to(inv, (RT, hd))
                if a == 0:
                    q_plain[rows, :] = normed.astype(BF16)
                    q_turned[:hd, rows] = jnp.transpose(normed).astype(BF16)
                else:
                    k_aug[rows, :hd] = normed.astype(BF16)
                    k_turned[:, rows] = jnp.transpose(normed).astype(BF16)
            g_turned[:, rows] = jnp.transpose(arrived(3).astype(F32)).astype(BF16)
            dk_acc[rows, :] = jnp.zeros((RT, hd), F32)
            dv_acc[rows, :] = jnp.zeros((RT, hd), F32)
            return c

        lax.fori_loop(0, length // RT, norm, 0)

        def panel(i, c):
            q_rows = pl.ds(pl.multiple_of(i * QT, QT), QT)
            q_tile = q_plain[q_rows, :]
            q_turn = q_turned[:, q_rows]
            g_turn = g_turned[:, q_rows]
            g_tile = in_buf[pl.ds(pl.multiple_of(base + 3 * length + i * QT, QT), QT), :]
            first = jnp.maximum(i * QT - (MOST - 1), 0) // KT
            last = jnp.minimum(i * QT + QT - 1 + MOST - 1, length - 1) // KT + 1

            def chunk(j):
                return pl.ds(pl.multiple_of(j * KT, KT), KT)

            def scores(j, top):
                rows = chunk(j)
                s = matmul(k_aug[rows, :], q_turn)
                s_buf[rows, :] = s
                v = in_buf[pl.ds(pl.multiple_of(base + 2 * length + j * KT, KT), KT), :]
                w_buf[rows, :] = matmul(v, g_turn)
                return jnp.maximum(top, jnp.max(fold(s), axis=0))

            top = lax.fori_loop(first, last, scores, jnp.full((8, QT), -jnp.inf, F32))
            top = jnp.max(top, axis=0, keepdims=True)

            def exps(j, total):
                rows = chunk(j)
                e = jnp.exp2((s_buf[rows, :] - top) * exponent)
                s_buf[rows, :] = e
                return total + jnp.sum(fold(e), axis=0)

            total = lax.fori_loop(first, last, exps, jnp.zeros((8, QT), F32))
            over = 1.0 / jnp.sum(total, axis=0, keepdims=True)

            def weights(j, delta):
                rows = chunk(j)
                w = s_buf[rows, :] * over
                s_buf[rows, :] = w
                p = w.astype(BF16)
                p_buf[rows, :] = p
                return delta + jnp.sum(fold(p.astype(F32) * w_buf[rows, :]), axis=0)

            delta = lax.fori_loop(first, last, weights, jnp.zeros((8, QT), F32))
            delta = jnp.sum(delta, axis=0, keepdims=True)

            def grads(j, dq):
                rows = chunk(j)
                ds = (s_buf[rows, :] * (w_buf[rows, :] - delta)).astype(BF16)
                dv_acc[rows, :] += matmul(p_buf[rows, :], g_tile)
                dk_acc[rows, :] += matmul(ds, q_tile)
                return dq + matmul(k_turned[:, rows], ds)

            dq = lax.fori_loop(first, last, grads, jnp.zeros((hd, QT), F32))
            tangent = jnp.transpose(dq) * scaling
            unit = unit_buf[q_rows, :]
            out_rows = pl.ds(pl.multiple_of(out_base + i * QT, QT), QT)
            out_buf[out_rows, :] = norm_backward(
                tangent, unit, inv_buf[q_rows, :], gains_ref[0:1, :]
            )
            gain_acc[0:8, :] += jnp.sum(fold(tangent * unit), axis=0)
            return c

        lax.fori_loop(0, length // QT, panel, 0)

        def finish(t, c):
            rows = pl.ds(pl.multiple_of(t * RT, RT), RT)
            side_rows = pl.ds(pl.multiple_of(length + t * RT, RT), RT)
            tangent = dk_acc[rows, :] * scaling
            unit = unit_buf[side_rows, :]
            out_buf[pl.ds(pl.multiple_of(out_base + length + t * RT, RT), RT), :] = norm_backward(
                tangent, unit, inv_buf[side_rows, :], gains_ref[1:2, :]
            )
            gain_acc[8:16, :] += jnp.sum(fold(tangent * unit), axis=0)
            out_buf[pl.ds(pl.multiple_of(out_base + 2 * length + t * RT, RT), RT), :] = dv_acc[
                rows, :
            ].astype(BF16)
            return c

        lax.fori_loop(0, length // RT, finish, 0)

        @pl.when(h == heads - 1)
        def _():
            terms = [jnp.sum(gain_acc[8 * a : 8 * a + 8, :], axis=0, keepdims=True) for a in (0, 1)]
            own = jnp.concatenate(terms + [jnp.zeros((6, hd), F32)], axis=0)
            gain_acc[16:24, :] = own
            slot = pl.ds(pl.multiple_of(seq * 8, 8), 8)
            gain_seq[slot, :] = own

            def send_terms(i, c):
                remote(
                    gain_acc.at[pl.ds(16, 8)], gain_seq.at[slot],
                    gain_send.at[0], gain_recv.at[0], partner(i), mp,
                ).start()
                return c

            lax.fori_loop(1, n, send_terms, 0)

        targets = (oq_ref, ok_ref, ov_ref)

        def out_rows(a, s):
            return pl.ds(pl.multiple_of(((h * 3 + a) * n + s) * tok, tok), tok)

        for a in range(3):
            pltpu.make_async_copy(
                out_buf.at[out_rows(a, seq)], targets[a].at[:, lanes(seq, h)], out_recv.at[0]
            ).start()

            def send_one(i, c, a=a):
                to = partner(i)
                remote(
                    out_buf.at[out_rows(a, to)], targets[a].at[:, lanes(seq, h)],
                    out_send.at[0], out_recv.at[0], to, mp,
                ).start()
                return c

            lax.fori_loop(1, n, send_one, 0)
        return c

    lax.fori_loop(0, heads, one_head, 0)

    got = gain_seq.at[pl.ds(0, (n - 1) * 8)]
    pltpu.make_async_copy(got, got, gain_recv.at[0]).wait()
    row_sum = jnp.sum(gain_seq[...].reshape(n, 8, hd), axis=0)
    gain_acc[24:32, :] = row_sum
    mp_slot = pl.ds(pl.multiple_of(mp * 8, 8), 8)
    gain_mp[mp_slot, :] = row_sum

    def send_sums(i, c):
        remote(
            gain_acc.at[pl.ds(24, 8)], gain_mp.at[mp_slot],
            gain_send.at[1], gain_recv.at[1], seq, mp_partner(i),
        ).start()
        return c

    lax.fori_loop(1, m, send_sums, 0)
    got = gain_mp.at[pl.ds(0, (m - 1) * 8)]
    pltpu.make_async_copy(got, got, gain_recv.at[1]).wait()
    total = jnp.sum(gain_mp[...].reshape(m, 8, hd), axis=0)
    gain_ref[...] = total[:2] * (length * n * heads) ** (-0.5)

    def drain(ref, sem):
        pltpu.make_async_copy(ref, ref, sem).wait()

    drain(id_buf.at[pl.ds(0, (n - 1) * 8)], id_send.at[0])
    drain(gain_seq.at[pl.ds(0, (n - 1) * 8)], gain_send.at[0])
    drain(gain_mp.at[pl.ds(0, (m - 1) * 8)], gain_send.at[1])
    drain(in_buf.at[pl.ds(0, heads * 4 * (n - 1) * tok)], in_send.at[0])
    drain(out_buf.at[pl.ds(0, heads * 3 * (n - 1) * tok)], out_send.at[0])
    drain(out_buf, out_recv.at[0])


def settle(q_ref, k_ref, v_ref, gain_in, oq_hbm, ok_hbm, ov_hbm, gain_hbm, sems):
    parts = 4
    rows = q_ref.shape[0] // parts
    copies = [
        pltpu.make_async_copy(a.at[piece], b.at[0, piece], sems.at[parts * i + p])
        for i, (a, b) in enumerate(((q_ref, oq_hbm), (k_ref, ok_hbm), (v_ref, ov_hbm)))
        for p, piece in enumerate(pl.ds(p * rows, rows) for p in range(parts))
    ]
    copies.append(pltpu.make_async_copy(gain_in, gain_hbm, sems.at[3 * parts]))
    for copy in copies:
        copy.start()
    for copy in copies:
        copy.wait()


def shards(n, m, query_raw, key_raw, value_rows, out_grads, image_ids, qk_gains):
    tok, width = query_raw.shape[1:]
    hd = qk_gains.shape[1]
    heads = width // hd // n
    length = n * tok
    landed = pltpu.VMEM((tok, width), BF16)
    grad = jax.ShapeDtypeStruct(query_raw.shape, BF16)
    gain = jax.ShapeDtypeStruct((2, hd), F32)
    hbm = pl.BlockSpec(memory_space=pl.ANY)
    vmem = pl.BlockSpec(memory_space=pltpu.VMEM)
    dma = pltpu.SemaphoreType.DMA
    arrived = pl.pallas_call(
        functools.partial(kernel, n, m, heads, tok, hd),
        out_shape=(landed, landed, landed, pltpu.VMEM((2, hd), F32)),
        in_specs=[hbm, hbm, hbm, hbm, hbm, hbm],
        out_specs=(vmem, vmem, vmem, vmem),
        scratch_shapes=[
            pltpu.VMEM((heads * 4 * length, hd), BF16),
            pltpu.VMEM((heads * 3 * length, hd), BF16),
            pltpu.VMEM((1, tok), jnp.int32),
            pltpu.VMEM((2, hd), F32),
            pltpu.VMEM((8, tok), jnp.int32),
            pltpu.VMEM((n * 8, tok), jnp.int32),
            pltpu.VMEM((length, hd), BF16),
            pltpu.VMEM((2 * hd, length), BF16),
            pltpu.VMEM((hd, length), BF16),
            pltpu.VMEM((length, 2 * hd), BF16),
            pltpu.VMEM((hd, length), BF16),
            pltpu.VMEM((2 * length, hd), F32),
            pltpu.VMEM((2 * length, hd), F32),
            pltpu.VMEM((length, QT), F32),
            pltpu.VMEM((length, QT), F32),
            pltpu.VMEM((length, QT), BF16),
            pltpu.VMEM((length, hd), F32),
            pltpu.VMEM((length, hd), F32),
            pltpu.VMEM((32, hd), F32),
            pltpu.VMEM((n * 8, hd), F32),
            pltpu.VMEM((m * 8, hd), F32),
            dma((2,)), dma((1,)), dma((heads,)), dma((1,)), dma((1,)), dma((1,)), dma((1,)), dma((2,)), dma((2,)),
        ],
        compiler_params=pltpu.CompilerParams(
            collective_id=0, has_side_effects=True, vmem_limit_bytes=48 * 2**20
        ),
    )(
        query_raw, key_raw, value_rows, out_grads,
        pltpu.with_memory_space_constraint(image_ids, pltpu.HBM),
        pltpu.with_memory_space_constraint(qk_gains, pltpu.HBM),
    )
    return pl.pallas_call(
        settle,
        out_shape=(grad, grad, grad, gain),
        in_specs=[vmem, vmem, vmem, vmem],
        out_specs=(hbm, hbm, hbm, hbm),
        scratch_shapes=[dma((13,))],
        compiler_params=pltpu.CompilerParams(vmem_limit_bytes=2**20),
    )(*(pltpu.with_memory_space_constraint(a, pltpu.VMEM) for a in arrived))


def solution(mesh):
    rows = P("mp", "seq", None)
    return jax.shard_map(
        functools.partial(shards, mesh.shape["seq"], mesh.shape["mp"]),
        mesh=mesh,
        in_specs=(rows, rows, rows, rows, P("mp", "seq"), P()),
        out_specs=(rows, rows, rows, P()),
        check_vma=False,
    )
```

```python
import functools
import math

import jax
import jax.numpy as jnp
from jax import lax
from jax.experimental import pallas as pl
from jax.experimental.pallas import tpu as pltpu
from jax.sharding import PartitionSpec as P

MESH = pl.DeviceIdType.MESH
EPSILON = 1e-06
BAN = -32768.0
CLASSES = 8
QT = 512
KT = 2048
RT = 2048
MOST = 1024
F32 = jnp.float32
BF16 = jnp.bfloat16


def matmul(a, b):
    return lax.dot_general(a, b, (((1,), (0,)), ((), ())), preferred_element_type=F32)


def fold(x):
    return x.reshape(x.shape[0] // 8, 8, x.shape[1])


def kernel(
    n, m, heads, tok, hd,
    q_hbm, k_hbm, v_hbm, g_hbm, ids_hbm, gains_hbm,
    oq_ref, ok_ref, ov_ref, gain_ref,
    in_buf, out_buf, ids_ref, gains_ref, id_src, id_buf, q_plain, q_turned, g_turned, k_aug, k_turned, unit_buf, inv_buf,
    s_buf, w_buf, dk_acc, dv_acc, gain_acc, gain_seq, gain_mp,
    own_sems, in_send, in_recv, id_send, id_recv, out_send, out_recv, gain_send, gain_recv,
):
    seq, mp = lax.axis_index("seq"), lax.axis_index("mp")
    length = n * tok
    side = math.isqrt(n)
    scaling = hd ** (-0.5)
    exponent = scaling * math.log2(math.e)

    def partner(i):
        i = lax.rem(i * 7, n)
        z = lax.rem(seq // side + i // side, side)
        x = lax.rem(lax.rem(seq, side) + lax.rem(i, side), side)
        return z * side + x

    def mp_partner(i):
        return lax.rem(mp + i, m)

    def remote(src, dst, send, recv, to_seq, to_mp):
        return pltpu.make_async_remote_copy(
            src_ref=src, dst_ref=dst, send_sem=send, recv_sem=recv,
            device_id=(to_seq, to_mp), device_id_type=MESH,
        )

    own_ids = pltpu.make_async_copy(ids_hbm, ids_ref, own_sems.at[0])
    own_gains = pltpu.make_async_copy(gains_hbm, gains_ref, own_sems.at[1])
    own_ids.start()
    own_gains.start()
    barrier = pltpu.get_barrier_semaphore()

    def greet_seq(i, c):
        pl.semaphore_signal(barrier, inc=1, device_id=(partner(i), mp), device_id_type=MESH)
        return c

    def greet_mp(i, c):
        pl.semaphore_signal(barrier, inc=1, device_id=(seq, mp_partner(i)), device_id_type=MESH)
        return c

    lax.fori_loop(1, n, greet_seq, 0)
    lax.fori_loop(1, m, greet_mp, 0)
    own_ids.wait()
    own_gains.wait()
    id_src[...] = jnp.broadcast_to(ids_ref[...], (8, tok))
    id_buf[pl.ds(pl.multiple_of(seq * 8, 8), 8), :] = jnp.broadcast_to(ids_ref[...], (8, tok))
    pl.semaphore_wait(barrier, n - 1 + m - 1)

    def send_ids(i, c):
        remote(
            id_src, id_buf.at[pl.ds(pl.multiple_of(seq * 8, 8), 8)],
            id_send.at[0], id_recv.at[0], partner(i), mp,
        ).start()
        return c

    lax.fori_loop(1, n, send_ids, 0)
    sources = (q_hbm, k_hbm, v_hbm, g_hbm)

    def in_rows(h, a, s):
        return pl.ds(pl.multiple_of(((h * 4 + a) * n + s) * tok, tok), tok)

    def lanes(owner, h):
        return pl.ds(pl.multiple_of((owner * heads + h) * hd, hd), hd)

    def send_head(h, c):
        for a in range(4):
            pltpu.make_async_copy(
                sources[a].at[0, :, lanes(seq, h)], in_buf.at[in_rows(h, a, seq)], in_recv.at[h]
            ).start()

            def send_one(i, c, a=a):
                to = partner(i)
                remote(
                    sources[a].at[0, :, lanes(to, h)], in_buf.at[in_rows(h, a, seq)],
                    in_send.at[0], in_recv.at[h], to, mp,
                ).start()
                return c

            lax.fori_loop(1, n, send_one, 0)
        return c

    lax.fori_loop(0, heads, send_head, 0)

    ids_got = id_buf.at[pl.ds(0, (n - 1) * 8)]
    pltpu.make_async_copy(ids_got, ids_got, id_recv.at[0]).wait()
    lane = lax.broadcasted_iota(jnp.int32, (tok, hd), 1)
    level = lax.broadcasted_iota(jnp.int32, (hd, tok), 0)

    def features(s, c):
        row = id_buf[pl.ds(pl.multiple_of(s * 8, 8), 8), :].astype(F32)[:1]
        image = jnp.transpose(jnp.broadcast_to(row, (hd, tok))).astype(jnp.int32)
        rows = pl.ds(pl.multiple_of(s * tok, tok), tok)
        q_turned[hd:, rows] = jnp.where(row.astype(jnp.int32) == level, 1.0, 0.0).astype(BF16)
        k_aug[rows, hd:] = jnp.where(
            jnp.logical_and(lane < CLASSES, image != lane), BAN, 0.0
        ).astype(BF16)
        return c

    lax.fori_loop(0, n, features, 0)
    gain_acc[...] = jnp.zeros_like(gain_acc)

    def mean(x):
        return jnp.sum(x.astype(F32), axis=-1, keepdims=True) * (1.0 / hd)

    def norm_backward(tangent, unit, inv, gain_row):
        u = tangent * gain_row
        return (inv * (u - mean(u) - unit * mean(u * unit))).astype(BF16)

    def one_head(h, c):
        base = pl.multiple_of(h * 4 * length, tok)
        out_base = pl.multiple_of(h * 3 * length, tok)
        whole = in_buf.at[pl.ds(base, 4 * length)]
        pltpu.make_async_copy(whole, whole, in_recv.at[h]).wait()

        def norm(t, c):
            rows = pl.ds(pl.multiple_of(t * RT, RT), RT)

            def arrived(a):
                return in_buf[pl.ds(pl.multiple_of(base + a * length + t * RT, RT), RT), :]

            for a in (0, 1):
                side_rows = pl.ds(pl.multiple_of(a * length + t * RT, RT), RT)
                raw = arrived(a)
                centered = raw.astype(F32) - mean(raw)
                inv = lax.rsqrt(mean(centered * centered) + EPSILON)
                unit = centered * inv
                normed = unit * gains_ref[a : a + 1, :]
                unit_buf[side_rows, :] = unit
                inv_buf[side_rows, :] = jnp.broadcast_to(inv, (RT, hd))
                if a == 0:
                    q_plain[rows, :] = normed.astype(BF16)
                    q_turned[:hd, rows] = jnp.transpose(normed).astype(BF16)
                else:
                    k_aug[rows, :hd] = normed.astype(BF16)
                    k_turned[:, rows] = jnp.transpose(normed).astype(BF16)
            g_turned[:, rows] = jnp.transpose(arrived(3).astype(F32)).astype(BF16)
            dk_acc[rows, :] = jnp.zeros((RT, hd), F32)
            dv_acc[rows, :] = jnp.zeros((RT, hd), F32)
            return c

        lax.fori_loop(0, length // RT, norm, 0)

        def panel(i, c):
            q_rows = pl.ds(pl.multiple_of(i * QT, QT), QT)
            q_tile = q_plain[q_rows, :]
            q_turn = q_turned[:, q_rows]
            g_turn = g_turned[:, q_rows]
            g_tile = in_buf[pl.ds(pl.multiple_of(base + 3 * length + i * QT, QT), QT), :]
            first = jnp.maximum(i * QT - (MOST - 1), 0) // KT
            last = jnp.minimum(i * QT + QT - 1 + MOST - 1, length - 1) // KT + 1

            def chunk(j):
                return pl.ds(pl.multiple_of(j * KT, KT), KT)

            def scores(j, top):
                rows = chunk(j)
                s = matmul(k_aug[rows, :], q_turn)
                s_buf[rows, :] = s
                return jnp.maximum(top, jnp.max(fold(s), axis=0))

            top = lax.fori_loop(first, last, scores, jnp.full((8, QT), -jnp.inf, F32))
            top = jnp.max(top, axis=0, keepdims=True)

            def exps(j, total):
                rows = chunk(j)
                v = in_buf[pl.ds(pl.multiple_of(base + 2 * length + j * KT, KT), KT), :]
                w_buf[rows, :] = matmul(v, g_turn)
                e = jnp.exp2((s_buf[rows, :] - top) * exponent)
                s_buf[rows, :] = e
                return total + jnp.sum(fold(e), axis=0)

            total = lax.fori_loop(first, last, exps, jnp.zeros((8, QT), F32))
            over = 1.0 / jnp.sum(total, axis=0, keepdims=True)

            def weights(j, delta):
                rows = chunk(j)
                w = s_buf[rows, :] * over
                s_buf[rows, :] = w
                p = w.astype(BF16)
                dv_acc[rows, :] += matmul(p, g_tile)
                return delta + jnp.sum(fold(p.astype(F32) * w_buf[rows, :]), axis=0)

            delta = lax.fori_loop(first, last, weights, jnp.zeros((8, QT), F32))
            delta = jnp.sum(delta, axis=0, keepdims=True)

            def grads(j, dq):
                rows = chunk(j)
                ds = (s_buf[rows, :] * (w_buf[rows, :] - delta)).astype(BF16)
                dk_acc[rows, :] += matmul(ds, q_tile)
                return dq + matmul(k_turned[:, rows], ds)

            dq = lax.fori_loop(first, last, grads, jnp.zeros((hd, QT), F32))
            tangent = jnp.transpose(dq) * scaling
            unit = unit_buf[q_rows, :]
            out_rows = pl.ds(pl.multiple_of(out_base + i * QT, QT), QT)
            out_buf[out_rows, :] = norm_backward(
                tangent, unit, inv_buf[q_rows, :], gains_ref[0:1, :]
            )
            gain_acc[0:8, :] += jnp.sum(fold(tangent * unit), axis=0)
            return c

        lax.fori_loop(0, length // QT, panel, 0)

        def finish(t, c):
            rows = pl.ds(pl.multiple_of(t * RT, RT), RT)
            side_rows = pl.ds(pl.multiple_of(length + t * RT, RT), RT)
            tangent = dk_acc[rows, :] * scaling
            unit = unit_buf[side_rows, :]
            out_buf[pl.ds(pl.multiple_of(out_base + length + t * RT, RT), RT), :] = norm_backward(
                tangent, unit, inv_buf[side_rows, :], gains_ref[1:2, :]
            )
            gain_acc[8:16, :] += jnp.sum(fold(tangent * unit), axis=0)
            out_buf[pl.ds(pl.multiple_of(out_base + 2 * length + t * RT, RT), RT), :] = dv_acc[
                rows, :
            ].astype(BF16)
            return c

        lax.fori_loop(0, length // RT, finish, 0)

        @pl.when(h == heads - 1)
        def _():
            terms = [jnp.sum(gain_acc[8 * a : 8 * a + 8, :], axis=0, keepdims=True) for a in (0, 1)]
            own = jnp.concatenate(terms + [jnp.zeros((6, hd), F32)], axis=0)
            gain_acc[16:24, :] = own
            slot = pl.ds(pl.multiple_of(seq * 8, 8), 8)
            gain_seq[slot, :] = own

            def send_terms(i, c):
                remote(
                    gain_acc.at[pl.ds(16, 8)], gain_seq.at[slot],
                    gain_send.at[0], gain_recv.at[0], partner(i), mp,
                ).start()
                return c

            lax.fori_loop(1, n, send_terms, 0)

        targets = (oq_ref, ok_ref, ov_ref)

        def out_rows(a, s):
            return pl.ds(pl.multiple_of(((h * 3 + a) * n + s) * tok, tok), tok)

        for a in range(3):
            pltpu.make_async_copy(
                out_buf.at[out_rows(a, seq)], targets[a].at[:, lanes(seq, h)], out_recv.at[0]
            ).start()

            def send_one(i, c, a=a):
                to = partner(i)
                remote(
                    out_buf.at[out_rows(a, to)], targets[a].at[:, lanes(seq, h)],
                    out_send.at[0], out_recv.at[0], to, mp,
                ).start()
                return c

            lax.fori_loop(1, n, send_one, 0)
        return c

    lax.fori_loop(0, heads, one_head, 0)

    got = gain_seq.at[pl.ds(0, (n - 1) * 8)]
    pltpu.make_async_copy(got, got, gain_recv.at[0]).wait()
    row_sum = jnp.sum(gain_seq[...].reshape(n, 8, hd), axis=0)
    gain_acc[24:32, :] = row_sum
    mp_slot = pl.ds(pl.multiple_of(mp * 8, 8), 8)
    gain_mp[mp_slot, :] = row_sum

    def send_sums(i, c):
        remote(
            gain_acc.at[pl.ds(24, 8)], gain_mp.at[mp_slot],
            gain_send.at[1], gain_recv.at[1], seq, mp_partner(i),
        ).start()
        return c

    lax.fori_loop(1, m, send_sums, 0)
    got = gain_mp.at[pl.ds(0, (m - 1) * 8)]
    pltpu.make_async_copy(got, got, gain_recv.at[1]).wait()
    total = jnp.sum(gain_mp[...].reshape(m, 8, hd), axis=0)
    gain_ref[...] = total[:2] * (length * n * heads) ** (-0.5)

    def drain(ref, sem):
        pltpu.make_async_copy(ref, ref, sem).wait()

    drain(id_buf.at[pl.ds(0, (n - 1) * 8)], id_send.at[0])
    drain(gain_seq.at[pl.ds(0, (n - 1) * 8)], gain_send.at[0])
    drain(gain_mp.at[pl.ds(0, (m - 1) * 8)], gain_send.at[1])
    drain(in_buf.at[pl.ds(0, heads * 4 * (n - 1) * tok)], in_send.at[0])
    drain(out_buf.at[pl.ds(0, heads * 3 * (n - 1) * tok)], out_send.at[0])
    drain(out_buf, out_recv.at[0])


def settle(q_ref, k_ref, v_ref, gain_in, oq_hbm, ok_hbm, ov_hbm, gain_hbm, sems):
    parts = 2
    rows = q_ref.shape[0] // parts
    copies = [
        pltpu.make_async_copy(a.at[piece], b.at[0, piece], sems.at[parts * i + p])
        for i, (a, b) in enumerate(((q_ref, oq_hbm), (k_ref, ok_hbm), (v_ref, ov_hbm)))
        for p, piece in enumerate(pl.ds(p * rows, rows) for p in range(parts))
    ]
    copies.append(pltpu.make_async_copy(gain_in, gain_hbm, sems.at[3 * parts]))
    for copy in copies:
        copy.start()
    for copy in copies:
        copy.wait()


def shards(n, m, query_raw, key_raw, value_rows, out_grads, image_ids, qk_gains):
    tok, width = query_raw.shape[1:]
    hd = qk_gains.shape[1]
    heads = width // hd // n
    length = n * tok
    landed = pltpu.VMEM((tok, width), BF16)
    grad = jax.ShapeDtypeStruct(query_raw.shape, BF16)
    gain = jax.ShapeDtypeStruct((2, hd), F32)
    hbm = pl.BlockSpec(memory_space=pl.ANY)
    vmem = pl.BlockSpec(memory_space=pltpu.VMEM)
    dma = pltpu.SemaphoreType.DMA
    arrived = pl.pallas_call(
        functools.partial(kernel, n, m, heads, tok, hd),
        out_shape=(landed, landed, landed, pltpu.VMEM((2, hd), F32)),
        in_specs=[hbm, hbm, hbm, hbm, hbm, hbm],
        out_specs=(vmem, vmem, vmem, vmem),
        scratch_shapes=[
            pltpu.VMEM((heads * 4 * length, hd), BF16),
            pltpu.VMEM((heads * 3 * length, hd), BF16),
            pltpu.VMEM((1, tok), jnp.int32),
            pltpu.VMEM((2, hd), F32),
            pltpu.VMEM((8, tok), jnp.int32),
            pltpu.VMEM((n * 8, tok), jnp.int32),
            pltpu.VMEM((length, hd), BF16),
            pltpu.VMEM((2 * hd, length), BF16),
            pltpu.VMEM((hd, length), BF16),
            pltpu.VMEM((length, 2 * hd), BF16),
            pltpu.VMEM((hd, length), BF16),
            pltpu.VMEM((2 * length, hd), F32),
            pltpu.VMEM((2 * length, hd), F32),
            pltpu.VMEM((length, QT), F32),
            pltpu.VMEM((length, QT), F32),
            pltpu.VMEM((length, hd), F32),
            pltpu.VMEM((length, hd), F32),
            pltpu.VMEM((32, hd), F32),
            pltpu.VMEM((n * 8, hd), F32),
            pltpu.VMEM((m * 8, hd), F32),
            dma((2,)), dma((1,)), dma((heads,)), dma((1,)), dma((1,)), dma((1,)), dma((1,)), dma((2,)), dma((2,)),
        ],
        compiler_params=pltpu.CompilerParams(
            collective_id=0, has_side_effects=True, vmem_limit_bytes=48 * 2**20
        ),
    )(
        query_raw, key_raw, value_rows, out_grads,
        pltpu.with_memory_space_constraint(image_ids, pltpu.HBM),
        pltpu.with_memory_space_constraint(qk_gains, pltpu.HBM),
    )
    return pl.pallas_call(
        settle,
        out_shape=(grad, grad, grad, gain),
        in_specs=[vmem, vmem, vmem, vmem],
        out_specs=(hbm, hbm, hbm, hbm),
        scratch_shapes=[dma((7,))],
        compiler_params=pltpu.CompilerParams(vmem_limit_bytes=2**20),
    )(*(pltpu.with_memory_space_constraint(a, pltpu.VMEM) for a in arrived))


def solution(mesh):
    rows = P("mp", "seq", None)
    return jax.shard_map(
        functools.partial(shards, mesh.shape["seq"], mesh.shape["mp"]),
        mesh=mesh,
        in_specs=(rows, rows, rows, rows, P("mp", "seq"), P()),
        out_specs=(rows, rows, rows, P()),
        check_vma=False,
    )
```
